32 devices in a mesh: req: 8 (over z, y), tp: 4 (over x, core).
Axes of the slice: x: 2, y: 2, z: 4, core: 2. Of those that a mesh axis runs over, the one named last changes fastest.
Arguments:
- hidden_in: bfloat16 [2048, 2048], P('req'), may hold values from -40 to 40
- recompute_pos: int32 [8, 256], replicated, may hold values from 0 to 16383, as said below
- req_lengths: int32 [8], replicated, may hold values from 1 to 32, as said below
- stretch_order: int32 [8, 32], replicated, may hold values from 0 to 255, as said below
- page_table: int32 [2, 256], replicated, may hold values from 0 to 31, as said below
- cached_key_pool: bfloat16 [256, 512, 1024], P('req', None, 'tp'), may hold values from -6 to 6
- cached_value_pool: bfloat16 [256, 512, 1024], P('req', None, 'tp'), may hold values from -6 to 6
- attn_gain: float32 [2048], replicated, may hold values from 0.5 to 2
- w_query: bfloat16 [2048, 2048], P(None, 'tp'), may hold values from -1 to 1
- w_key: bfloat16 [2048, 1024], P(None, 'tp'), may hold values from -1 to 1
- value_weight: bfloat16 [2048, 1024], P(None, 'tp'), may hold values from -0.125 to 0.125
- query_gain: float32 [128], replicated, may hold values from 0 to 20
- key_norm_gain: float32 [128], replicated, may hold values from 0 to 20
- w_out: bfloat16 [2048, 2048], P('tp'), may hold values from -0.5 to 0.5
- ffn_gain: float32 [2048], replicated, may hold values from 0.5 to 2
- w_gate: bfloat16 [2048, 6144], P(None, 'tp'), may hold values from -0.125 to 0.125
- w_up: bfloat16 [2048, 6144], P(None, 'tp'), may hold values from -0.125 to 0.125
- w_down: bfloat16 [6144, 2048], P('tp'), may hold values from -0.078125 to 0.078125
Outputs:
- layer_out: bfloat16 [2048, 2048], P('req')
The draws below stay inside these ranges and needn't reach their ends.
Inputs may be any that keep to these rules, and one draw needn't show every extreme that they name: `req_lengths`: on each draw, the requests of one index along req (chosen anew each time) all have 32 stretches; the others have 1 to 32. `stretch_order`: every stretch id appears exactly once over all requests and places, places at or past a request's length included. `page_table`: every slot of every index along req holds exactly one stretch id, and each index holds exactly 4 of the 32 ids listed by the requests of any one index. `recompute_pos`: strictly increasing along a request, below 512 times the request's length; every request recomputes its first and its last position.
All inputs are finite; a program needn't handle non-finite values.
Results may differ from the reference program's by a relative error of at most 0.015.
The reference program's roundings to bfloat16 on the way count: a program that leaves them out, or rounds other values in their place, can miss the bound.
Values may be sent and summed in bfloat16 or wider, within the bound.
A program may use at most 256 MiB of HBM per device.

```python
import math
import jax
import jax.numpy as jnp
from jax import lax

MODEL_WIDTH = 2048
QUERY_HEADS = 16
KV_HEAD_COUNT = 8
HEAD_SIZE = 128
FF = 6144
STRETCH_TOKENS = 512
MOST_STRETCHES = 32
REQ_DEV = 1
RECOMPUTE_TOKENS = 256
REQUEST_COUNT = 8
TOKENS = 2048
POOL_SLOTS = 32
N_REQ = 8
N_TP = 4


def routing(key):
    base_key = jax.random.fold_in(key, 7001)
    length_key, full_key, offset_key, shuffle_key, stretch_key = jax.random.split(base_key, 5)
    dev_count = REQUEST_COUNT // REQ_DEV
    owner_dev = jnp.arange(REQUEST_COUNT) // REQ_DEV
    lengths = jax.random.randint(length_key, (REQUEST_COUNT,), 1, MOST_STRETCHES + 1)
    full_dev = jax.random.randint(full_key, (), 0, dev_count)
    lengths = jnp.where(owner_dev == full_dev, MOST_STRETCHES, lengths).astype(jnp.int32)
    order_scores = jax.random.randint(offset_key, (dev_count, POOL_SLOTS), 0, 2 ** 16) * POOL_SLOTS + jnp.arange(POOL_SLOTS)[None, :]
    offset = jnp.argsort(order_scores, axis=1).astype(jnp.int32)
    requester = jnp.arange(dev_count)[:, None]
    holder = (requester + offset) % dev_count
    base_slot = requester * (POOL_SLOTS // dev_count) + offset // dev_count
    shuffle_scores = jax.random.randint(shuffle_key, (dev_count, POOL_SLOTS), 0, 2 ** 16) * POOL_SLOTS + jnp.arange(POOL_SLOTS)[None, :]
    shuffle = jnp.argsort(shuffle_scores, axis=1).astype(jnp.int32)
    slot_index = shuffle[holder, base_slot]
    id_count = REQUEST_COUNT * MOST_STRETCHES
    id_scores = jax.random.randint(stretch_key, (id_count,), 0, 2 ** 12) * id_count + jnp.arange(id_count)
    stretch_ids = jnp.argsort(id_scores).astype(jnp.int32)
    page_rows = jnp.zeros((2, id_count), jnp.int32)
    page_rows = page_rows.at[0, stretch_ids].set(holder.reshape(id_count).astype(jnp.int32))
    page_rows = page_rows.at[1, stretch_ids].set(slot_index.reshape(id_count).astype(jnp.int32))
    return (lengths, stretch_ids.reshape(REQUEST_COUNT, MOST_STRETCHES), page_rows)


def positions(key, lengths):
    pos_key = jax.random.fold_in(key, 7002)
    span = MOST_STRETCHES * STRETCH_TOKENS
    place = jnp.arange(span)
    scores = jax.random.randint(pos_key, (REQUEST_COUNT, span), 0, 2 ** 14) * span + place[None, :]
    limit = lengths[:, None] * STRETCH_TOKENS
    scores = jnp.where(place[None, :] >= limit, -1, scores)
    scores = jnp.where((place[None, :] == 0) | (place[None, :] == limit - 1), 2 ** 30, scores)
    chosen = lax.top_k(scores, RECOMPUTE_TOKENS)[1]
    return jnp.sort(chosen, axis=1).astype(jnp.int32)


def draw_req_lengths(key, part):
    return routing(key)[0]


def draw_stretch_order(key, part):
    return routing(key)[1]


def draw_page_table(key, part):
    return routing(key)[2]


def draw_recompute_pos(key, part):
    return positions(key, routing(key)[0])


def draw_hidden_in(key, part):
    base_key = jax.random.fold_in(key, 7101)
    value_key = jax.random.fold_in(base_key, 0)
    row_key = jax.random.fold_in(base_key, 1)
    col_key = jax.random.fold_in(base_key, 2)
    near_key = jax.random.fold_in(base_key, 4)
    pair_count = TOKENS // 2
    row_scale = jnp.exp(jax.random.uniform(row_key, (pair_count, 1), minval=math.log(0.3), maxval=math.log(3.0)))
    col_scale = jnp.exp(jax.random.uniform(col_key, (1, MODEL_WIDTH), minval=math.log(0.3), maxval=math.log(3.0)))
    lead_rows = jax.random.normal(value_key, (pair_count, MODEL_WIDTH))
    near_rows = jax.random.normal(near_key, (pair_count, MODEL_WIDTH))
    paired = jnp.stack([lead_rows * row_scale, near_rows * row_scale], axis=1).reshape(TOKENS, MODEL_WIDTH)
    return jnp.clip(paired * col_scale, -40.0, 40.0).astype(jnp.bfloat16)


def weight_pair(key):
    base_key = jax.random.fold_in(key, 7201)
    query_key, key_random_seed = jax.random.split(base_key, 2)
    spread_width = MODEL_WIDTH ** (-0.5)
    query_matrix = jax.random.normal(query_key, (MODEL_WIDTH, QUERY_HEADS * HEAD_SIZE)) * spread_width
    key_matrix = jax.random.normal(key_random_seed, (MODEL_WIDTH, KV_HEAD_COUNT * HEAD_SIZE)) * spread_width
    return (jnp.clip(query_matrix, -1.0, 1.0), jnp.clip(key_matrix, -1.0, 1.0))


def draw_w_query(key, part):
    return weight_pair(key)[0].astype(jnp.bfloat16)


def draw_w_key(key, part):
    return weight_pair(key)[1].astype(jnp.bfloat16)


def gain_pair(key):
    base_key = jax.random.fold_in(key, 7301)
    query_key, key_random_seed = jax.random.split(base_key)
    query_scale = jnp.exp(jax.random.uniform(query_key, (HEAD_SIZE,), minval=math.log(1.2), maxval=math.log(3.0)))
    key_scale = jnp.exp(jax.random.uniform(key_random_seed, (HEAD_SIZE,), minval=math.log(0.7), maxval=math.log(1.4)))
    return (query_scale, key_scale)


def draw_query_gain(key, part):
    return gain_pair(key)[0].astype(jnp.float32)


def draw_key_norm_gain(key, part):
    return gain_pair(key)[1].astype(jnp.float32)


def level_of(stream_key, shape, pieces, low, top_value):
    factor_of, own = 1.0, jax.random.fold_in(stream_key, 6)
    for axis_at, shards_of in pieces:
        draws = jnp.exp(jax.random.uniform(jax.random.fold_in(own, axis_at), (shards_of,), jnp.float32, low / len(pieces), top_value / len(pieces)))
        factor_of = factor_of * jnp.repeat(draws, shape[axis_at] // shards_of).reshape([-1 if axis == axis_at else 1 for axis in range(len(shape))])
    return factor_of


def scatter_about(key, dims, width, bound, cuts=(), kind=jnp.bfloat16):
    values = jax.random.normal(key, dims, jnp.float32) * width
    if len(cuts) > 0:
        values = level_of(key, dims, cuts, -0.22, 0.18) * values
    return jnp.clip(values, min=-bound, max=bound).astype(kind)


def setup_inputs(seed: int = 0) -> dict:
    streams_of = jax.random.split(jax.random.key(seed), 19)
    hidden_in = draw_hidden_in(jax.random.fold_in(streams_of[18], 71), 0)
    recompute_pos = draw_recompute_pos(jax.random.fold_in(streams_of[18], 71), 0)
    req_lengths = draw_req_lengths(jax.random.fold_in(streams_of[18], 71), 0)
    stretch_order = draw_stretch_order(jax.random.fold_in(streams_of[18], 71), 0)
    page_table = draw_page_table(jax.random.fold_in(streams_of[18], 71), 0)
    cached_key_pool = scatter_about(streams_of[5], (N_REQ * POOL_SLOTS, STRETCH_TOKENS, KV_HEAD_COUNT * HEAD_SIZE), 1.0, 6.0, ((0, 8), (2, 4)))
    cached_value_pool = scatter_about(streams_of[6], (N_REQ * POOL_SLOTS, STRETCH_TOKENS, KV_HEAD_COUNT * HEAD_SIZE), 1.0, 6.0, ((0, 8), (2, 4)))
    attn_gain = jnp.clip(jnp.exp(jax.random.uniform(streams_of[7], (MODEL_WIDTH,), jnp.float32, math.log(0.5), math.log(2.0))), 0.5, 2.0)
    w_query = draw_w_query(jax.random.fold_in(streams_of[18], 71), 0)
    w_key = draw_w_key(jax.random.fold_in(streams_of[18], 71), 0)
    value_weight = scatter_about(streams_of[10], (MODEL_WIDTH, KV_HEAD_COUNT * HEAD_SIZE), MODEL_WIDTH ** -0.5, 0.125, ((1, 4),))
    query_gain = draw_query_gain(jax.random.fold_in(streams_of[18], 71), 0)
    key_norm_gain = draw_key_norm_gain(jax.random.fold_in(streams_of[18], 71), 0)
    w_out = scatter_about(streams_of[13], (QUERY_HEADS * HEAD_SIZE, MODEL_WIDTH), HEAD_SIZE ** -0.5, 0.5, ((0, 4),))
    ffn_gain = jnp.clip(jnp.exp(jax.random.uniform(streams_of[14], (MODEL_WIDTH,), jnp.float32, math.log(0.5), math.log(2.0))), 0.5, 2.0)
    w_gate = scatter_about(streams_of[15], (MODEL_WIDTH, FF), MODEL_WIDTH ** -0.5, 0.125, ((1, 4),))
    w_up = scatter_about(streams_of[16], (MODEL_WIDTH, FF), MODEL_WIDTH ** -0.5, 0.125, ((1, 4),))
    w_down = scatter_about(streams_of[17], (FF, MODEL_WIDTH), FF ** -0.5, 0.078125, ((0, 4),))
    return {"hidden_in": hidden_in, "recompute_pos": recompute_pos, "req_lengths": req_lengths, "stretch_order": stretch_order, "page_table": page_table, "cached_key_pool": cached_key_pool, "cached_value_pool": cached_value_pool, "attn_gain": attn_gain, "w_query": w_query, "w_key": w_key, "value_weight": value_weight, "query_gain": query_gain, "key_norm_gain": key_norm_gain, "w_out": w_out, "ffn_gain": ffn_gain, "w_gate": w_gate, "w_up": w_up, "w_down": w_down}


eps_norm = 1e-06
rope_base = 1000000.0
floor_score = -1e+30

def norm_rows(matrix, gain_vec):
    wide = matrix.astype(jnp.float32)
    factor = lax.rsqrt(lax.optimization_barrier(jnp.mean(wide * wide, axis=-1, keepdims=True)) + eps_norm)
    return wide * factor * gain_vec

def angles(position, head_size):
    half_dim = head_size // 2
    frequency = rope_base ** (-jnp.arange(half_dim, dtype=jnp.float32) / half_dim)
    return position.astype(jnp.float32)[..., None] * frequency

def rotate_halves(vector, angle_arg):
    half_dim = vector.shape[-1] // 2
    lower_half = vector[..., :half_dim]
    upper_half = vector[..., half_dim:]
    cosine = jnp.cos(angle_arg)
    sine_part = jnp.sin(angle_arg)
    return jnp.concatenate([lower_half * cosine - upper_half * sine_part, upper_half * cosine + lower_half * sine_part], axis=-1)

def rotary_heads(raw_proj, gain_vec, position, head_count):
    split_heads = raw_proj.reshape(raw_proj.shape[0], head_count, HEAD_SIZE)
    normed = norm_rows(split_heads, gain_vec)
    return rotate_halves(normed, angles(position, HEAD_SIZE)[:, None, :]).astype(jnp.bfloat16)

def block_stats(grouped_heads, gathered_stretch_keys, values, live_mask):
    scores = jnp.einsum('mhgd,khd->hgmk', grouped_heads.astype(jnp.float32), gathered_stretch_keys.astype(jnp.float32)) * HEAD_SIZE ** (-0.5)
    row_peak = lax.optimization_barrier(jnp.max(jnp.where(live_mask, scores, floor_score), axis=-1))
    weights = jnp.where(live_mask, jnp.exp(scores - row_peak[..., None]), 0.0)
    weight_sum = lax.optimization_barrier(jnp.sum(weights, axis=-1))
    rounded = lax.optimization_barrier(weights.astype(jnp.bfloat16))
    weighted = jnp.einsum('hgmk,khd->hgmd', rounded.astype(jnp.float32), values.astype(jnp.float32))
    return (weighted, row_peak, weight_sum)

def attend(query_tensor, position, length, gathered_stretch_keys, gathered_stretch_values, recomputed_keys, recomputed_values):
    count_of_rows = query_tensor.shape[0]
    grouped_heads = query_tensor.reshape(count_of_rows, KV_HEAD_COUNT, QUERY_HEADS // KV_HEAD_COUNT, HEAD_SIZE)
    key_place = jnp.arange(MOST_STRETCHES * STRETCH_TOKENS)
    live_mask = (key_place[None, :] < position[:, None]) & (key_place[None, :] // STRETCH_TOKENS < length)
    own_mask = position[None, :] <= position[:, None]
    cached_sum, cached_peak, cached_total = block_stats(grouped_heads, gathered_stretch_keys, gathered_stretch_values, live_mask)
    fresh_sum, fresh_peak, fresh_total = block_stats(grouped_heads, recomputed_keys, recomputed_values, own_mask)
    row_top = jnp.maximum(cached_peak, fresh_peak)
    cached_factor = jnp.exp(cached_peak - row_top)
    fresh_factor = jnp.exp(fresh_peak - row_top)
    weighted = cached_sum * cached_factor[..., None] + fresh_sum * fresh_factor[..., None]
    weight_sum = cached_total * cached_factor + fresh_total * fresh_factor
    result = weighted / weight_sum[..., None]
    return result.transpose(2, 0, 1, 3).astype(jnp.bfloat16).reshape(count_of_rows, QUERY_HEADS * HEAD_SIZE)

def group_sum(left_mat, right_mat):
    count_of_rows = left_mat.shape[0]
    terms = jnp.einsum('tnc,ncd->ntd', left_mat.reshape(count_of_rows, N_TP, -1).astype(jnp.float32), right_mat.reshape(N_TP, -1, right_mat.shape[1]).astype(jnp.float32))
    terms = lax.optimization_barrier(terms.astype(jnp.bfloat16))
    return lax.optimization_barrier(jnp.sum(terms.astype(jnp.float32), axis=0))

def reference(hidden_in, recompute_pos, req_lengths, stretch_order, page_table, cached_key_pool, cached_value_pool, attn_gain, w_query, w_key, value_weight, query_gain, key_norm_gain, w_out, ffn_gain, w_gate, w_up, w_down):
    normed = norm_rows(hidden_in, attn_gain).astype(jnp.bfloat16)
    query_raw = jnp.dot(normed, w_query, preferred_element_type=jnp.float32)
    unnormed_keys = jnp.dot(normed, w_key, preferred_element_type=jnp.float32)
    recomputed_values = jnp.dot(normed, value_weight, preferred_element_type=jnp.float32).astype(jnp.bfloat16)
    flattened_position = recompute_pos.reshape(TOKENS)
    queries = rotary_heads(query_raw, query_gain, flattened_position, QUERY_HEADS).reshape(REQUEST_COUNT, RECOMPUTE_TOKENS, QUERY_HEADS, HEAD_SIZE)
    recomputed_keys = rotary_heads(unnormed_keys, key_norm_gain, flattened_position, KV_HEAD_COUNT).reshape(REQUEST_COUNT, RECOMPUTE_TOKENS, KV_HEAD_COUNT, HEAD_SIZE)
    recomputed_values = recomputed_values.reshape(REQUEST_COUNT, RECOMPUTE_TOKENS, KV_HEAD_COUNT, HEAD_SIZE)
    pool_index = (page_table[0] * POOL_SLOTS + page_table[1]).astype(jnp.int32)
    position_shift_angle = angles(jnp.arange(MOST_STRETCHES) * STRETCH_TOKENS, HEAD_SIZE)[:, None, None, :]

    def one_request(packed):
        query_tensor, fkeys, fvalues, position, length, order = packed
        index_value = pool_index[order]
        gathered_stretch_keys = cached_key_pool[index_value].reshape(MOST_STRETCHES, STRETCH_TOKENS, KV_HEAD_COUNT, HEAD_SIZE).astype(jnp.float32)
        gathered_stretch_keys = rotate_halves(gathered_stretch_keys, position_shift_angle).astype(jnp.bfloat16).reshape(MOST_STRETCHES * STRETCH_TOKENS, KV_HEAD_COUNT, HEAD_SIZE)
        gathered_stretch_values = cached_value_pool[index_value].reshape(MOST_STRETCHES * STRETCH_TOKENS, KV_HEAD_COUNT, HEAD_SIZE)
        return attend(query_tensor, position, length, gathered_stretch_keys, gathered_stretch_values, fkeys, fvalues)
    attended = lax.map(one_request, (queries, recomputed_keys, recomputed_values, recompute_pos, req_lengths, stretch_order))
    attended = attended.reshape(TOKENS, QUERY_HEADS * HEAD_SIZE)
    attn_out = group_sum(attended, w_out)
    residual = (hidden_in.astype(jnp.float32) + attn_out).astype(jnp.bfloat16)
    normed_ffn = norm_rows(residual, ffn_gain).astype(jnp.bfloat16)
    gate_proj = jnp.dot(normed_ffn, w_gate, preferred_element_type=jnp.float32)
    up_proj = jnp.dot(normed_ffn, w_up, preferred_element_type=jnp.float32)
    hidden = (jax.nn.silu(gate_proj) * up_proj).astype(jnp.bfloat16)
    return (residual.astype(jnp.float32) + group_sum(hidden, w_down)).astype(jnp.bfloat16)
```

```python
import jax
import jax.numpy as jnp
from jax import lax
from jax.experimental import pallas as pl
from jax.experimental.pallas import tpu as pltpu
from jax.sharding import PartitionSpec as P

STRETCH_TOKENS = 512
MOST_STRETCHES = 32
REQ_DEV = 1
RECOMPUTE_TOKENS = 256


eps_norm = 1e-06
rope_base = 1000000.0
floor_score = -1e30
start_peak = -1e29
LOG2E = 1.4426950408889634
CHUNK = 128


def held_kernel(slot_ref, place_ref, first_ref, q_ref, k_ref, v_ref, pos_ref, cos_ref, sin_ref,
                o_ref, lse_ref, acc, peak, total):
    req, rank = pl.program_id(0), pl.program_id(1)
    ranks = pl.num_programs(1)
    head = cos_ref.shape[1]
    heads = k_ref.shape[2] // head
    groups = q_ref.shape[2] // head // heads
    chunks = q_ref.shape[1] // CHUNK
    tokens = k_ref.shape[1]
    scale = head ** (-0.5) * LOG2E

    @pl.when(rank == 0)
    def _():
        acc[...] = jnp.zeros_like(acc)
        peak[...] = jnp.full_like(peak, start_peak)
        total[...] = jnp.zeros_like(total)

    step = req * ranks + rank
    place = place_ref[step]
    first = first_ref[step]

    @pl.when(first < chunks * CHUNK)
    def _():
        cosine = cos_ref[pl.ds(place, 1), :]
        sine = sin_ref[pl.ds(place, 1), :]
        rotated = []
        for h in range(heads):
            wide = k_ref[0, :, h * head:(h + 1) * head].astype(jnp.float32)
            turned = pltpu.roll(wide, head // 2, 1)
            rotated.append((wide * cosine + turned * sine).astype(jnp.bfloat16))
        where_key = place * tokens + lax.broadcasted_iota(
            jnp.int32, (tokens, groups * CHUNK), 0
        )
        for c in range(chunks):
            @pl.when(first < (c + 1) * CHUNK)
            def _():
                row = pos_ref[0, :, c * CHUNK:(c + 1) * CHUNK]
                live = where_key < jnp.concatenate([row] * groups, axis=1)
                for h in range(heads):
                    at = h * chunks + c
                    query = jnp.concatenate(
                        [
                            q_ref[0, c * CHUNK:(c + 1) * CHUNK,
                                  (h * groups + g) * head:(h * groups + g + 1) * head]
                            for g in range(groups)
                        ],
                        axis=0,
                    )
                    scores = lax.dot_general(
                        rotated[h], query, (((1,), (1,)), ((), ())),
                        preferred_element_type=jnp.float32,
                    )
                    scores = jnp.where(live, scores * scale, floor_score)
                    old = peak[at]
                    new = jnp.maximum(old, jnp.max(scores, axis=0, keepdims=True))
                    weights = jnp.exp2(scores - new)
                    factor = jnp.exp2(old - new)
                    peak[at] = new
                    total[at] = total[at] * factor + jnp.sum(weights, axis=0, keepdims=True)
                    acc[at] = acc[at] * factor + lax.dot_general(
                        v_ref[0, :, h * head:(h + 1) * head], weights.astype(jnp.bfloat16),
                        (((0,), (0,)), ((), ())), preferred_element_type=jnp.float32,
                    )

    @pl.when(rank == ranks - 1)
    def _():
        for h in range(heads):
            for c in range(chunks):
                at = h * chunks + c
                some = total[at]
                held = some > 0.0
                safe = jnp.where(held, some, 1.0)
                out = (acc[at] / safe).T.astype(o_ref.dtype)
                for g in range(groups):
                    o_ref[0, c * CHUNK:(c + 1) * CHUNK,
                          (h * groups + g) * head:(h * groups + g + 1) * head] = out[
                        g * CHUNK:(g + 1) * CHUNK]
                lse_ref[0, at:at + 1, :] = jnp.where(held, peak[at] + jnp.log2(safe), start_peak)


def held_attention(q_all, slots, places, firsts, key_pool, value_pool, positions, cosines, sines):
    reqs, rows, width = q_all.shape
    ranks = slots.shape[0] // reqs
    tokens, kv_width = key_pool.shape[1:]
    head = cosines.shape[1]
    heads = kv_width // head
    groups = width // kv_width
    chunks = rows // CHUNK
    pool = pl.BlockSpec((1, tokens, kv_width), lambda r, j, s, p, f: (s[r * ranks + j], 0, 0))
    whole_table = pl.BlockSpec(cosines.shape, lambda r, j, s, p, f: (0, 0))
    return pl.pallas_call(
        held_kernel,
        grid_spec=pltpu.PrefetchScalarGridSpec(
            num_scalar_prefetch=3,
            grid=(reqs, ranks),
            in_specs=[
                pl.BlockSpec((1, rows, width), lambda r, j, s, p, f: (r, 0, 0)),
                pool,
                pool,
                pl.BlockSpec((1, 1, rows), lambda r, j, s, p, f: (r, 0, 0)),
                whole_table,
                whole_table,
            ],
            out_specs=[
                pl.BlockSpec((1, rows, width), lambda r, j, s, p, f: (r, 0, 0)),
                pl.BlockSpec((1, heads * chunks, groups * CHUNK), lambda r, j, s, p, f: (r, 0, 0)),
            ],
            scratch_shapes=[
                pltpu.VMEM((heads * chunks, head, groups * CHUNK), jnp.float32),
                pltpu.VMEM((heads * chunks, 1, groups * CHUNK), jnp.float32),
                pltpu.VMEM((heads * chunks, 1, groups * CHUNK), jnp.float32),
            ],
        ),
        out_shape=[
            jax.ShapeDtypeStruct((reqs, rows, width), jnp.bfloat16),
            jax.ShapeDtypeStruct((reqs, heads * chunks, groups * CHUNK), jnp.float32),
        ],
        compiler_params=pltpu.CompilerParams(
            dimension_semantics=("arbitrary", "arbitrary"), vmem_limit_bytes=32 * 1024 * 1024
        ),
        name="held_attention",
    )(slots, places, firsts, q_all, key_pool, value_pool, positions, cosines, sines)


def norm_rows(matrix, gain_vec):
    wide = matrix.astype(jnp.float32)
    factor = lax.rsqrt(jnp.mean(wide * wide, axis=-1, keepdims=True) + eps_norm)
    return wide * factor * gain_vec


def angles(position, head_size):
    half_dim = head_size // 2
    frequency = rope_base ** (-jnp.arange(half_dim, dtype=jnp.float32) / half_dim)
    return position.astype(jnp.float32)[..., None] * frequency


def rotate_halves(vector, angle_arg):
    half_dim = vector.shape[-1] // 2
    lower_half = vector[..., :half_dim]
    upper_half = vector[..., half_dim:]
    cosine = jnp.cos(angle_arg)
    sine_part = jnp.sin(angle_arg)
    return jnp.concatenate(
        [
            lower_half * cosine - upper_half * sine_part,
            upper_half * cosine + lower_half * sine_part,
        ],
        axis=-1,
    )


def rotary_heads(raw_proj, gain_vec, position, head_count):
    head_size = gain_vec.shape[0]
    split_heads = raw_proj.reshape(raw_proj.shape[0], head_count, head_size)
    normed = norm_rows(split_heads, gain_vec)
    return rotate_halves(normed, angles(position, head_size)[:, None, :]).astype(jnp.bfloat16)


def block_stats(grouped_heads, gathered_stretch_keys, values, live_mask):
    count_of_rows, key_heads, groups, head_size = grouped_heads.shape
    scores = jnp.einsum(
        "mhgd,khd->hgmk", grouped_heads, gathered_stretch_keys, preferred_element_type=jnp.float32
    ) * head_size ** (-0.5)
    row_peak = jnp.max(jnp.where(live_mask, scores, floor_score), axis=-1)
    weights = jnp.where(live_mask, jnp.exp(scores - row_peak[..., None]), 0.0)
    weight_sum = jnp.sum(weights, axis=-1)
    weighted = jnp.einsum(
        "hgmk,khd->mhgd", weights.astype(jnp.bfloat16), values, preferred_element_type=jnp.float32
    )
    head_total = key_heads * groups
    return (
        weighted.reshape(count_of_rows, head_total, head_size),
        row_peak.transpose(2, 0, 1).reshape(count_of_rows, head_total),
        weight_sum.transpose(2, 0, 1).reshape(count_of_rows, head_total),
    )


def swiglu(rows_in, w_gate, w_up):
    gate_proj = jnp.dot(rows_in, w_gate, preferred_element_type=jnp.float32)
    up_proj = jnp.dot(rows_in, w_up, preferred_element_type=jnp.float32)
    return (jax.nn.silu(gate_proj) * up_proj).astype(jnp.bfloat16)


def on_device(
    hidden_in,
    recompute_pos,
    req_lengths,
    stretch_order,
    page_table,
    cached_key_pool,
    cached_value_pool,
    attn_gain,
    w_query,
    w_key,
    value_weight,
    query_gain,
    key_norm_gain,
    w_out,
    ffn_gain,
    w_gate,
    w_up,
    w_down,
):
    req_count = lax.axis_size("req")
    my_index = lax.axis_index("req")
    head_size = query_gain.shape[0]
    query_heads = w_query.shape[1] // head_size
    key_heads = w_key.shape[1] // head_size
    groups = query_heads // key_heads
    count_of_rows = hidden_in.shape[0]
    local_reqs = REQ_DEV
    req_rows = RECOMPUTE_TOKENS
    entries = local_reqs * MOST_STRETCHES
    pair_cap = entries // req_count
    normed = norm_rows(hidden_in, attn_gain).astype(jnp.bfloat16)
    query_raw = jnp.dot(normed, w_query, preferred_element_type=jnp.float32)
    unnormed_keys = jnp.dot(normed, w_key, preferred_element_type=jnp.float32)
    recomputed_values = (
        jnp.dot(normed, value_weight, preferred_element_type=jnp.float32)
        .astype(jnp.bfloat16)
        .reshape(count_of_rows, key_heads, head_size)
    )
    my_positions = lax.dynamic_slice_in_dim(recompute_pos, my_index * local_reqs, local_reqs, 0)
    my_lengths = lax.dynamic_slice_in_dim(req_lengths, my_index * local_reqs, local_reqs, 0)
    flattened_position = my_positions.reshape(count_of_rows)
    queries = rotary_heads(query_raw, query_gain, flattened_position, query_heads)
    recomputed_keys = rotary_heads(unnormed_keys, key_norm_gain, flattened_position, key_heads)
    grouped_heads = queries.reshape(count_of_rows, key_heads, groups, head_size)
    row_owner = jnp.arange(count_of_rows) // req_rows
    own_mask = (row_owner[None, :] == row_owner[:, None]) & (
        flattened_position[None, :] <= flattened_position[:, None]
    )
    fresh_sum, fresh_peak, fresh_total = block_stats(
        grouped_heads, recomputed_keys, recomputed_values, own_mask
    )
    holder_table = page_table[0][stretch_order]
    slot_table = page_table[1][stretch_order]
    holder_hits = holder_table[:, :, None] == jnp.arange(req_count)[None, None, :]
    hit_counts = jnp.cumsum(holder_hits.astype(jnp.int32), axis=1)
    pair_rank = jnp.sum(jnp.where(holder_hits, hit_counts - 1, 0), axis=2)
    my_sends = (holder_table == my_index)[:, :, None] & (
        pair_rank[:, :, None] == jnp.arange(pair_cap)[None, None, :]
    )
    send_slot = jnp.sum(jnp.where(my_sends, slot_table[:, :, None], 0), axis=1)
    place_ids = jnp.arange(MOST_STRETCHES)[None, :, None]
    send_place = jnp.sum(jnp.where(my_sends, place_ids, 0), axis=1)
    below = jnp.sum(
        (recompute_pos[:, None, :] <= (send_place * STRETCH_TOKENS)[:, :, None]).astype(jnp.int32),
        axis=2,
    )
    first_row = jnp.where(send_place < req_lengths[:, None], below, req_rows)
    shift_angle = angles(jnp.arange(MOST_STRETCHES) * STRETCH_TOKENS, head_size)
    cosine, sine = jnp.cos(shift_angle), jnp.sin(shift_angle)
    queries_all = lax.all_gather(
        queries.reshape(count_of_rows, query_heads * head_size), "req", axis=0
    )
    held_out, held_lse = held_attention(
        queries_all,
        send_slot.reshape(-1),
        send_place.reshape(-1),
        first_row.reshape(-1),
        cached_key_pool,
        cached_value_pool,
        recompute_pos.reshape(req_count, 1, req_rows),
        jnp.concatenate([cosine, cosine], axis=1),
        jnp.concatenate([-sine, sine], axis=1),
    )
    got_out = lax.all_to_all(held_out, "req", split_axis=0, concat_axis=0, tiled=True)
    got_lse = lax.all_to_all(held_lse, "req", split_axis=0, concat_axis=0, tiled=True)
    chunks = req_rows // CHUNK
    got_lse = (
        got_lse.reshape(req_count, key_heads, chunks, groups, CHUNK)
        .transpose(0, 2, 4, 1, 3)
        .reshape(req_count, count_of_rows, query_heads)
    )
    row_top = jnp.maximum(jnp.max(got_lse, axis=0), fresh_peak * LOG2E)
    held_factor = jnp.exp2(got_lse - row_top[None])
    fresh_factor = jnp.exp2(fresh_peak * LOG2E - row_top)
    weighted = fresh_sum * fresh_factor[..., None] + jnp.sum(
        got_out.reshape(req_count, count_of_rows, query_heads, head_size).astype(jnp.float32)
        * held_factor[..., None],
        axis=0,
    )
    total = fresh_total * fresh_factor + jnp.sum(held_factor, axis=0)
    attended = (weighted / total[..., None]).astype(jnp.bfloat16).reshape(count_of_rows, -1)
    attn_out = lax.psum(
        jnp.dot(attended, w_out, preferred_element_type=jnp.float32).astype(jnp.bfloat16), "tp"
    ).astype(jnp.float32)
    residual = (hidden_in.astype(jnp.float32) + attn_out).astype(jnp.bfloat16)
    normed_ffn = norm_rows(residual, ffn_gain).astype(jnp.bfloat16)
    hidden = swiglu(normed_ffn, w_gate, w_up)
    ffn_out = lax.psum(
        jnp.dot(hidden, w_down, preferred_element_type=jnp.float32).astype(jnp.bfloat16), "tp"
    ).astype(jnp.float32)
    return (residual.astype(jnp.float32) + ffn_out).astype(jnp.bfloat16)


def solution(mesh):
    return jax.shard_map(
        on_device,
        mesh=mesh,
        in_specs=(
            P("req", None),
            P(),
            P(),
            P(),
            P(),
            P("req", None, "tp"),
            P("req", None, "tp"),
            P(),
            P(None, "tp"),
            P(None, "tp"),
            P(None, "tp"),
            P(),
            P(),
            P("tp", None),
            P(),
            P(None, "tp"),
            P(None, "tp"),
            P("tp", None),
        ),
        out_specs=P("req", None),
        check_vma=False,
    )
```

```python
import functools

import jax
import jax.numpy as jnp
from jax import lax
from jax.experimental import pallas as pl
from jax.experimental.pallas import tpu as pltpu
from jax.sharding import PartitionSpec as P

STRETCH_TOKENS = 512
MOST_STRETCHES = 32
REQ_DEV = 1
RECOMPUTE_TOKENS = 256


eps_norm = 1e-06
rope_base = 1000000.0
floor_score = -1e30
start_peak = -1e29
LOG2E = 1.4426950408889634
CHUNK = 128
LSE_ROWS = 8
MESH = pl.DeviceIdType.MESH


def held_kernel(slot_ref, place_ref, first_ref, q_ref, k_ref, v_ref, pos_ref, cos_ref, sin_ref,
                o_ref, lse_ref, acc, peak, total):
    req, rank = pl.program_id(0), pl.program_id(1)
    ranks = pl.num_programs(1)
    head = cos_ref.shape[1]
    heads = k_ref.shape[2] // head
    groups = q_ref.shape[2] // head // heads
    chunks = q_ref.shape[1] // CHUNK
    tokens = k_ref.shape[1]
    scale = head ** (-0.5) * LOG2E

    @pl.when(rank == 0)
    def _():
        acc[...] = jnp.zeros_like(acc)
        peak[...] = jnp.full_like(peak, start_peak)
        total[...] = jnp.zeros_like(total)

    step = req * ranks + rank
    place = place_ref[step]
    first = first_ref[step]

    @pl.when(first < chunks * CHUNK)
    def _():
        cosine = cos_ref[pl.ds(place, 1), :]
        sine = sin_ref[pl.ds(place, 1), :]
        rotated = []
        for h in range(heads):
            wide = k_ref[0, :, h * head:(h + 1) * head].astype(jnp.float32)
            turned = pltpu.roll(wide, head // 2, 1)
            rotated.append((wide * cosine + turned * sine).astype(jnp.bfloat16))
        where_key = place * tokens + lax.broadcasted_iota(
            jnp.int32, (tokens, groups * CHUNK), 0
        )
        for c in range(chunks):
            @pl.when(first < (c + 1) * CHUNK)
            def _():
                row = pos_ref[0, :, c * CHUNK:(c + 1) * CHUNK]
                live = where_key < jnp.concatenate([row] * groups, axis=1)
                for h in range(heads):
                    at = h * chunks + c
                    query = jnp.concatenate(
                        [
                            q_ref[0, c * CHUNK:(c + 1) * CHUNK,
                                  (h * groups + g) * head:(h * groups + g + 1) * head]
                            for g in range(groups)
                        ],
                        axis=0,
                    )
                    scores = lax.dot_general(
                        rotated[h], query, (((1,), (1,)), ((), ())),
                        preferred_element_type=jnp.float32,
                    )
                    scores = jnp.where(live, scores * scale, floor_score)
                    old = peak[at]
                    new = jnp.maximum(old, jnp.max(scores, axis=0, keepdims=True))
                    weights = jnp.exp2(scores - new)
                    factor = jnp.exp2(old - new)
                    peak[at] = new
                    total[at] = total[at] * factor + jnp.sum(weights, axis=0, keepdims=True)
                    acc[at] = acc[at] * factor + lax.dot_general(
                        v_ref[0, :, h * head:(h + 1) * head], weights.astype(jnp.bfloat16),
                        (((0,), (0,)), ((), ())), preferred_element_type=jnp.float32,
                    )

    @pl.when(rank == ranks - 1)
    def _():
        lse_rows = []
        for h in range(heads):
            for c in range(chunks):
                at = h * chunks + c
                some = total[at]
                held = some > 0.0
                safe = jnp.where(held, some, 1.0)
                out = (acc[at] / safe).T.astype(o_ref.dtype)
                for g in range(groups):
                    o_ref[0, c * CHUNK:(c + 1) * CHUNK,
                          (h * groups + g) * head:(h * groups + g + 1) * head] = out[
                        g * CHUNK:(g + 1) * CHUNK]
                lse_rows.append(jnp.where(held, peak[at] + jnp.log2(safe), start_peak))
        lse_ref[0] = jnp.concatenate(
            lse_rows + [jnp.zeros_like(lse_rows[0])] * (LSE_ROWS - len(lse_rows)), axis=0
        )


def held_attention(q_all, slots, places, firsts, key_pool, value_pool, positions, cosines, sines):
    reqs, rows, width = q_all.shape
    ranks = slots.shape[0] // reqs
    tokens, kv_width = key_pool.shape[1:]
    head = cosines.shape[1]
    heads = kv_width // head
    groups = width // kv_width
    chunks = rows // CHUNK
    pool = pl.BlockSpec((1, tokens, kv_width), lambda r, j, s, p, f: (s[r * ranks + j], 0, 0))
    whole_table = pl.BlockSpec(cosines.shape, lambda r, j, s, p, f: (0, 0))
    return pl.pallas_call(
        held_kernel,
        grid_spec=pltpu.PrefetchScalarGridSpec(
            num_scalar_prefetch=3,
            grid=(reqs, ranks),
            in_specs=[
                pl.BlockSpec((1, rows, width), lambda r, j, s, p, f: (r, 0, 0)),
                pool,
                pool,
                pl.BlockSpec((1, 1, rows), lambda r, j, s, p, f: (r, 0, 0)),
                whole_table,
                whole_table,
            ],
            out_specs=[
                pl.BlockSpec((1, rows, width), lambda r, j, s, p, f: (r, 0, 0)),
                pl.BlockSpec((1, LSE_ROWS, groups * CHUNK), lambda r, j, s, p, f: (r, 0, 0)),
            ],
            scratch_shapes=[
                pltpu.VMEM((heads * chunks, head, groups * CHUNK), jnp.float32),
                pltpu.VMEM((heads * chunks, 1, groups * CHUNK), jnp.float32),
                pltpu.VMEM((heads * chunks, 1, groups * CHUNK), jnp.float32),
            ],
        ),
        out_shape=[
            jax.ShapeDtypeStruct((reqs, rows, width), jnp.bfloat16),
            jax.ShapeDtypeStruct((reqs, LSE_ROWS, groups * CHUNK), jnp.float32),
        ],
        compiler_params=pltpu.CompilerParams(
            dimension_semantics=("arbitrary", "arbitrary"), vmem_limit_bytes=32 * 1024 * 1024
        ),
        name="held_attention",
    )(slots, places, firsts, q_all, key_pool, value_pool, positions, cosines, sines)


def norm_rows(matrix, gain_vec):
    wide = matrix.astype(jnp.float32)
    factor = lax.rsqrt(jnp.mean(wide * wide, axis=-1, keepdims=True) + eps_norm)
    return wide * factor * gain_vec


def angles(position, head_size):
    half_dim = head_size // 2
    frequency = rope_base ** (-jnp.arange(half_dim, dtype=jnp.float32) / half_dim)
    return position.astype(jnp.float32)[..., None] * frequency


def rotate_halves(vector, angle_arg):
    half_dim = vector.shape[-1] // 2
    lower_half = vector[..., :half_dim]
    upper_half = vector[..., half_dim:]
    cosine = jnp.cos(angle_arg)
    sine_part = jnp.sin(angle_arg)
    return jnp.concatenate(
        [
            lower_half * cosine - upper_half * sine_part,
            upper_half * cosine + lower_half * sine_part,
        ],
        axis=-1,
    )


def rotary_heads(raw_proj, gain_vec, position, head_count):
    head_size = gain_vec.shape[0]
    split_heads = raw_proj.reshape(raw_proj.shape[0], head_count, head_size)
    normed = norm_rows(split_heads, gain_vec)
    return rotate_halves(normed, angles(position, head_size)[:, None, :]).astype(jnp.bfloat16)


def merge_kernel(head, heads, groups, out_ref, lse_ref, q_ref, k_ref, v_ref, row_ref, col_ref,
                 done_ref, got_out, got_lse, fresh_acc, fresh_peak, fresh_total, merged,
                 send_out, recv_out, send_lse, recv_lse):
    n = out_ref.shape[0]
    me = lax.axis_index("req")
    chunks = q_ref.shape[0] // CHUNK
    scale = head ** (-0.5) * LOG2E

    barrier = pltpu.get_barrier_semaphore()
    for d in range(1, n):
        pl.semaphore_signal(
            barrier, inc=1, device_id={"req": lax.rem(me + d, n)}, device_id_type=MESH
        )
    pl.semaphore_wait(barrier, n - 1)

    copies = []
    for d in range(1, n):
        other = lax.rem(me + d, n)
        small = pltpu.make_async_remote_copy(
            src_ref=lse_ref.at[other], dst_ref=got_lse.at[d - 1], send_sem=send_lse.at[d - 1],
            recv_sem=recv_lse.at[d - 1], device_id={"req": other}, device_id_type=MESH,
        )
        small.start()
        copies.append(small)
    outs = []
    for d in range(1, n):
        other = lax.rem(me + d, n)
        large = pltpu.make_async_remote_copy(
            src_ref=out_ref.at[other], dst_ref=got_out.at[d - 1], send_sem=send_out.at[d - 1],
            recv_sem=recv_out.at[d - 1], device_id={"req": other}, device_id_type=MESH,
        )
        large.start()
        outs.append(large)

    for c in range(chunks):
        row = row_ref[:, c * CHUNK:(c + 1) * CHUNK]
        live = col_ref[...] <= jnp.concatenate([row] * groups, axis=1)
        for h in range(heads):
            at = h * chunks + c
            query = jnp.concatenate(
                [
                    q_ref[c * CHUNK:(c + 1) * CHUNK,
                          (h * groups + g) * head:(h * groups + g + 1) * head]
                    for g in range(groups)
                ],
                axis=0,
            )
            scores = lax.dot_general(
                k_ref[:, h * head:(h + 1) * head], query, (((1,), (1,)), ((), ())),
                preferred_element_type=jnp.float32,
            )
            scores = jnp.where(live, scores * scale, floor_score)
            top = jnp.max(scores, axis=0, keepdims=True)
            weights = jnp.exp2(scores - top)
            fresh_peak[at] = top
            fresh_total[at] = jnp.sum(weights, axis=0, keepdims=True)
            fresh_acc[at] = lax.dot_general(
                v_ref[:, h * head:(h + 1) * head], weights.astype(jnp.bfloat16),
                (((0,), (0,)), ((), ())), preferred_element_type=jnp.float32,
            )

    for small in copies:
        small.wait_recv()
    own_lse = lse_ref[me]
    columns = {}
    for h in range(heads):
        for c in range(chunks):
            at = h * chunks + c
            rows = [own_lse[at:at + 1, :]] + [got_lse[d - 1, at:at + 1, :] for d in range(1, n)]
            top = fresh_peak[at]
            for one in rows:
                top = jnp.maximum(top, one)
            fresh_factor = jnp.exp2(fresh_peak[at] - top)
            factors = [jnp.exp2(one - top) for one in rows]
            total = fresh_total[at] * fresh_factor
            for one in factors:
                total = total + one
            inverse = 1.0 / total
            stacked = jnp.concatenate(
                [one * inverse for one in factors]
                + [jnp.zeros((CHUNK - n, groups * CHUNK), jnp.float32)],
                axis=0,
            )
            columns[at] = stacked.T
            fresh = (fresh_acc[at] * (fresh_factor * inverse)).T
            for g in range(groups):
                at_rows = slice(c * CHUNK, (c + 1) * CHUNK)
                at_cols = slice((h * groups + g) * head, (h * groups + g + 1) * head)
                merged[at_rows, at_cols] = fresh[g * CHUNK:(g + 1) * CHUNK] + out_ref[
                    me, at_rows, at_cols
                ].astype(jnp.float32) * columns[at][g * CHUNK:(g + 1) * CHUNK, 0:1]
    for d in range(1, n):
        outs[d - 1].wait_recv()
        for h in range(heads):
            for c in range(chunks):
                at = h * chunks + c
                for g in range(groups):
                    at_rows = slice(c * CHUNK, (c + 1) * CHUNK)
                    at_cols = slice((h * groups + g) * head, (h * groups + g + 1) * head)
                    merged[at_rows, at_cols] += got_out[d - 1, at_rows, at_cols].astype(
                        jnp.float32
                    ) * columns[at][g * CHUNK:(g + 1) * CHUNK, d:d + 1]
    done_ref[...] = merged[...].astype(done_ref.dtype)
    for copy in copies + outs:
        copy.wait_send()


def exchange_and_merge(held_out, held_lse, queries, keys, values, position, head):
    n, rows, width = held_out.shape
    heads = keys.shape[1] // head
    groups = width // keys.shape[1]
    pairs = heads * (rows // CHUNK)
    vmem = pl.BlockSpec(memory_space=pltpu.VMEM)
    return pl.pallas_call(
        functools.partial(merge_kernel, head, heads, groups),
        out_shape=jax.ShapeDtypeStruct((rows, width), jnp.bfloat16),
        in_specs=[vmem] * 7,
        out_specs=vmem,
        scratch_shapes=[
            pltpu.VMEM((n - 1, rows, width), jnp.bfloat16),
            pltpu.VMEM((n - 1,) + held_lse.shape[1:], jnp.float32),
            pltpu.VMEM((pairs, head, groups * CHUNK), jnp.float32),
            pltpu.VMEM((pairs, 1, groups * CHUNK), jnp.float32),
            pltpu.VMEM((pairs, 1, groups * CHUNK), jnp.float32),
            pltpu.VMEM((rows, width), jnp.float32),
        ]
        + [pltpu.SemaphoreType.DMA((n - 1,))] * 4,
        compiler_params=pltpu.CompilerParams(
            collective_id=0, has_side_effects=True, vmem_limit_bytes=40 * 1024 * 1024
        ),
        name="exchange_and_merge",
    )(held_out, held_lse, queries, keys, values, position[None, :], position[:, None])


def group_sum_kernel(term_ref, base_ref, out_ref, pair_in, chip_sum, cross_in,
                     send_pair, recv_pair, send_cross, recv_cross, send_own, recv_own,
                     send_pass, recv_pass):
    chips = chip_sum.shape[0]
    rows = term_ref.shape[0]
    half = rows // 2
    part = half // chips
    me = lax.axis_index("tp")
    core = lax.rem(me, 2)
    chip = me // 2
    sibling = chip * 2 + 1 - core

    def same_core(d):
        return lax.rem(chip + d, chips)

    def rows_of(core_at, chip_at):
        return pl.ds(pl.multiple_of(core_at * half + chip_at * part, part), part)

    barrier = pltpu.get_barrier_semaphore()
    for d in range(1, chips):
        pl.semaphore_signal(
            barrier, inc=1, device_id={"tp": same_core(d) * 2 + core}, device_id_type=MESH
        )
    pl.semaphore_signal(barrier, inc=1, device_id={"tp": sibling}, device_id_type=MESH)
    pl.semaphore_wait(barrier, chips)

    order = list(range(1, chips)) + [0]
    pair = {}
    for d in order:
        chip_at = same_core(d)
        pair[d] = pltpu.make_async_remote_copy(
            src_ref=term_ref.at[rows_of(1 - core, chip_at)], dst_ref=pair_in.at[d],
            send_sem=send_pair.at[d], recv_sem=recv_pair.at[d],
            device_id={"tp": sibling}, device_id_type=MESH,
        )
        pair[d].start()
    cross = {}
    for d in range(1, chips):
        chip_at = same_core(d)
        pair[d].wait_recv()
        chip_sum[d] = (
            term_ref[rows_of(core, chip_at), :].astype(jnp.float32)
            + pair_in[d].astype(jnp.float32)
        ).astype(chip_sum.dtype)
        cross[d] = pltpu.make_async_remote_copy(
            src_ref=chip_sum.at[d], dst_ref=cross_in.at[d],
            send_sem=send_cross.at[d], recv_sem=recv_cross.at[d],
            device_id={"tp": chip_at * 2 + core}, device_id_type=MESH,
        )
        cross[d].start()
    pair[0].wait_recv()
    mine = rows_of(core, chip)
    summed = term_ref[mine, :].astype(jnp.float32) + pair_in[0].astype(jnp.float32)
    for d in range(1, chips):
        cross[d].wait_recv()
        summed = summed + cross_in[d].astype(jnp.float32)
    out_ref[mine, :] = (base_ref[mine, :].astype(jnp.float32) + summed).astype(out_ref.dtype)
    own = []
    for d in range(1, chips):
        own.append(
            pltpu.make_async_remote_copy(
                src_ref=out_ref.at[mine], dst_ref=out_ref.at[mine],
                send_sem=send_own.at[d], recv_sem=recv_own.at[d],
                device_id={"tp": same_core(d) * 2 + core}, device_id_type=MESH,
            )
        )
        own[-1].start()
    passed = []
    for d in range(chips):
        if d > 0:
            own[d - 1].wait_recv()
        come = rows_of(core, lax.rem(chip - d + chips, chips))
        passed.append(
            pltpu.make_async_remote_copy(
                src_ref=out_ref.at[come], dst_ref=out_ref.at[come],
                send_sem=send_pass.at[d], recv_sem=recv_pass.at[d],
                device_id={"tp": sibling}, device_id_type=MESH,
            )
        )
        passed[-1].start()
    for copy in passed:
        copy.wait_recv()
    for copy in list(pair.values()) + list(cross.values()) + own + passed:
        copy.wait_send()


def add_group_sum(term, base, collective_id):
    chips = lax.axis_size("tp") // 2
    rows, width = term.shape
    part = rows // 2 // chips
    vmem = pl.BlockSpec(memory_space=pltpu.VMEM)
    return pl.pallas_call(
        group_sum_kernel,
        out_shape=jax.ShapeDtypeStruct((rows, width), jnp.bfloat16),
        in_specs=[vmem] * 2,
        out_specs=vmem,
        scratch_shapes=[pltpu.VMEM((chips, part, width), jnp.bfloat16)] * 3
        + [pltpu.SemaphoreType.DMA((chips,))] * 8,
        compiler_params=pltpu.CompilerParams(
            collective_id=collective_id, has_side_effects=True, vmem_limit_bytes=32 * 1024 * 1024
        ),
        name="add_group_sum",
    )(term, base)


def swiglu(rows_in, w_gate, w_up):
    gate_proj = jnp.dot(rows_in, w_gate, preferred_element_type=jnp.float32)
    up_proj = jnp.dot(rows_in, w_up, preferred_element_type=jnp.float32)
    return (jax.nn.silu(gate_proj) * up_proj).astype(jnp.bfloat16)


def on_device(
    hidden_in,
    recompute_pos,
    req_lengths,
    stretch_order,
    page_table,
    cached_key_pool,
    cached_value_pool,
    attn_gain,
    w_query,
    w_key,
    value_weight,
    query_gain,
    key_norm_gain,
    w_out,
    ffn_gain,
    w_gate,
    w_up,
    w_down,
):
    req_count = lax.axis_size("req")
    my_index = lax.axis_index("req")
    head_size = query_gain.shape[0]
    query_heads = w_query.shape[1] // head_size
    key_heads = w_key.shape[1] // head_size
    count_of_rows = hidden_in.shape[0]
    local_reqs = REQ_DEV
    req_rows = RECOMPUTE_TOKENS
    entries = local_reqs * MOST_STRETCHES
    pair_cap = entries // req_count
    normed = norm_rows(hidden_in, attn_gain).astype(jnp.bfloat16)
    query_raw = jnp.dot(normed, w_query, preferred_element_type=jnp.float32)
    unnormed_keys = jnp.dot(normed, w_key, preferred_element_type=jnp.float32)
    recomputed_values = (
        jnp.dot(normed, value_weight, preferred_element_type=jnp.float32)
        .astype(jnp.bfloat16)
    )
    my_positions = lax.dynamic_slice_in_dim(recompute_pos, my_index * local_reqs, local_reqs, 0)
    flattened_position = my_positions.reshape(count_of_rows)
    queries = rotary_heads(query_raw, query_gain, flattened_position, query_heads)
    recomputed_keys = rotary_heads(unnormed_keys, key_norm_gain, flattened_position, key_heads)
    holder_table = page_table[0][stretch_order]
    slot_table = page_table[1][stretch_order]
    holder_hits = holder_table[:, :, None] == jnp.arange(req_count)[None, None, :]
    hit_counts = jnp.cumsum(holder_hits.astype(jnp.int32), axis=1)
    pair_rank = jnp.sum(jnp.where(holder_hits, hit_counts - 1, 0), axis=2)
    my_sends = (holder_table == my_index)[:, :, None] & (
        pair_rank[:, :, None] == jnp.arange(pair_cap)[None, None, :]
    )
    send_slot = jnp.sum(jnp.where(my_sends, slot_table[:, :, None], 0), axis=1)
    place_ids = jnp.arange(MOST_STRETCHES)[None, :, None]
    send_place = jnp.sum(jnp.where(my_sends, place_ids, 0), axis=1)
    below = jnp.sum(
        (recompute_pos[:, None, :] <= (send_place * STRETCH_TOKENS)[:, :, None]).astype(jnp.int32),
        axis=2,
    )
    first_row = jnp.where(send_place < req_lengths[:, None], below, req_rows)
    shift_angle = angles(jnp.arange(MOST_STRETCHES) * STRETCH_TOKENS, head_size)
    cosine, sine = jnp.cos(shift_angle), jnp.sin(shift_angle)
    queries_all = lax.all_gather(
        queries.reshape(count_of_rows, query_heads * head_size), "req", axis=0
    )
    held_out, held_lse = held_attention(
        queries_all,
        send_slot.reshape(-1),
        send_place.reshape(-1),
        first_row.reshape(-1),
        cached_key_pool,
        cached_value_pool,
        recompute_pos.reshape(req_count, 1, req_rows),
        jnp.concatenate([cosine, cosine], axis=1),
        jnp.concatenate([-sine, sine], axis=1),
    )
    attended = exchange_and_merge(
        held_out,
        held_lse,
        queries.reshape(count_of_rows, query_heads * head_size),
        recomputed_keys.reshape(count_of_rows, key_heads * head_size),
        recomputed_values,
        flattened_position,
        head_size,
    )
    attn_term = jnp.dot(attended, w_out, preferred_element_type=jnp.float32).astype(jnp.bfloat16)
    residual = add_group_sum(attn_term, hidden_in, 1)
    normed_ffn = norm_rows(residual, ffn_gain).astype(jnp.bfloat16)
    hidden = swiglu(normed_ffn, w_gate, w_up)
    ffn_term = jnp.dot(hidden, w_down, preferred_element_type=jnp.float32).astype(jnp.bfloat16)
    return add_group_sum(ffn_term, residual, 2)


def solution(mesh):
    return jax.shard_map(
        on_device,
        mesh=mesh,
        in_specs=(
            P("req", None),
            P(),
            P(),
            P(),
            P(),
            P("req", None, "tp"),
            P("req", None, "tp"),
            P(),
            P(None, "tp"),
            P(None, "tp"),
            P(None, "tp"),
            P(),
            P(),
            P("tp", None),
            P(),
            P(None, "tp"),
            P(None, "tp"),
            P("tp", None),
        ),
        out_specs=P("req", None),
        check_vma=False,
    )
```

```python
import functools

import jax
import jax.numpy as jnp
from jax import lax
from jax.experimental import pallas as pl
from jax.experimental.pallas import tpu as pltpu
from jax.sharding import PartitionSpec as P

STRETCH_TOKENS = 512
MOST_STRETCHES = 32
REQ_DEV = 1
RECOMPUTE_TOKENS = 256


eps_norm = 1e-06
rope_base = 1000000.0
floor_score = -1e30
start_peak = -1e29
LOG2E = 1.4426950408889634
CHUNK = 128
LSE_ROWS = 8
MESH = pl.DeviceIdType.MESH


def held_kernel(slot_ref, place_ref, first_ref, q_ref, k_ref, v_ref, pos_ref, cos_ref, sin_ref,
                o_ref, lse_ref, acc, peak, total):
    req, rank = pl.program_id(0), pl.program_id(1)
    ranks = pl.num_programs(1)
    head = cos_ref.shape[1]
    heads = k_ref.shape[2] // head
    groups = q_ref.shape[2] // head // heads
    chunks = q_ref.shape[1] // CHUNK
    tokens = k_ref.shape[1]
    scale = head ** (-0.5) * LOG2E

    @pl.when(rank == 0)
    def _():
        acc[...] = jnp.zeros_like(acc)
        peak[...] = jnp.full_like(peak, start_peak)
        total[...] = jnp.zeros_like(total)

    step = req * ranks + rank
    place = place_ref[step]
    first = first_ref[step]

    @pl.when(first < chunks * CHUNK)
    def _():
        cosine = cos_ref[pl.ds(place, 1), :]
        sine = sin_ref[pl.ds(place, 1), :]
        rotated = []
        for h in range(heads):
            wide = k_ref[0, :, h * head:(h + 1) * head].astype(jnp.float32)
            turned = pltpu.roll(wide, head // 2, 1)
            rotated.append((wide * cosine + turned * sine).astype(jnp.bfloat16))
        where_key = place * tokens + lax.broadcasted_iota(
            jnp.int32, (tokens, groups * CHUNK), 0
        )
        for c in range(chunks):
            @pl.when(first < (c + 1) * CHUNK)
            def _():
                row = pos_ref[0, :, c * CHUNK:(c + 1) * CHUNK]
                live = where_key < jnp.concatenate([row] * groups, axis=1)
                for h in range(heads):
                    at = h * chunks + c
                    query = jnp.concatenate(
                        [
                            q_ref[0, c * CHUNK:(c + 1) * CHUNK,
                                  (h * groups + g) * head:(h * groups + g + 1) * head]
                            for g in range(groups)
                        ],
                        axis=0,
                    )
                    scores = lax.dot_general(
                        rotated[h], query, (((1,), (1,)), ((), ())),
                        preferred_element_type=jnp.float32,
                    )
                    scores = jnp.where(live, scores * scale, floor_score)
                    old = peak[at]
                    new = jnp.maximum(old, jnp.max(scores, axis=0, keepdims=True))
                    weights = jnp.exp2(scores - new)
                    factor = jnp.exp2(old - new)
                    peak[at] = new
                    total[at] = total[at] * factor + jnp.sum(weights, axis=0, keepdims=True)
                    acc[at] = acc[at] * factor + lax.dot_general(
                        v_ref[0, :, h * head:(h + 1) * head], weights.astype(jnp.bfloat16),
                        (((0,), (0,)), ((), ())), preferred_element_type=jnp.float32,
                    )

    @pl.when(rank == ranks - 1)
    def _():
        lse_rows = []
        for h in range(heads):
            for c in range(chunks):
                at = h * chunks + c
                some = total[at]
                held = some > 0.0
                safe = jnp.where(held, some, 1.0)
                out = (acc[at] / safe).T.astype(o_ref.dtype)
                for g in range(groups):
                    o_ref[0, c * CHUNK:(c + 1) * CHUNK,
                          (h * groups + g) * head:(h * groups + g + 1) * head] = out[
                        g * CHUNK:(g + 1) * CHUNK]
                lse_rows.append(jnp.where(held, peak[at] + jnp.log2(safe), start_peak))
        lse_ref[0] = jnp.concatenate(
            lse_rows + [jnp.zeros_like(lse_rows[0])] * (LSE_ROWS - len(lse_rows)), axis=0
        )


def held_attention(q_all, slots, places, firsts, key_pool, value_pool, positions, cosines, sines):
    reqs, rows, width = q_all.shape
    ranks = slots.shape[0] // reqs
    tokens, kv_width = key_pool.shape[1:]
    head = cosines.shape[1]
    heads = kv_width // head
    groups = width // kv_width
    chunks = rows // CHUNK
    pool = pl.BlockSpec((1, tokens, kv_width), lambda r, j, s, p, f: (s[r * ranks + j], 0, 0))
    whole_table = pl.BlockSpec(cosines.shape, lambda r, j, s, p, f: (0, 0))
    return pl.pallas_call(
        held_kernel,
        grid_spec=pltpu.PrefetchScalarGridSpec(
            num_scalar_prefetch=3,
            grid=(reqs, ranks),
            in_specs=[
                pl.BlockSpec((1, rows, width), lambda r, j, s, p, f: (r, 0, 0)),
                pool,
                pool,
                pl.BlockSpec((1, 1, rows), lambda r, j, s, p, f: (r, 0, 0)),
                whole_table,
                whole_table,
            ],
            out_specs=[
                pl.BlockSpec((1, rows, width), lambda r, j, s, p, f: (r, 0, 0)),
                pl.BlockSpec((1, LSE_ROWS, groups * CHUNK), lambda r, j, s, p, f: (r, 0, 0)),
            ],
            scratch_shapes=[
                pltpu.VMEM((heads * chunks, head, groups * CHUNK), jnp.float32),
                pltpu.VMEM((heads * chunks, 1, groups * CHUNK), jnp.float32),
                pltpu.VMEM((heads * chunks, 1, groups * CHUNK), jnp.float32),
            ],
        ),
        out_shape=[
            jax.ShapeDtypeStruct((reqs, rows, width), jnp.bfloat16),
            jax.ShapeDtypeStruct((reqs, LSE_ROWS, groups * CHUNK), jnp.float32),
        ],
        compiler_params=pltpu.CompilerParams(
            dimension_semantics=("arbitrary", "arbitrary"), vmem_limit_bytes=56 * 1024 * 1024
        ),
        name="held_attention",
    )(slots, places, firsts, q_all, key_pool, value_pool, positions, cosines, sines)


def norm_rows(matrix, gain_vec):
    wide = matrix.astype(jnp.float32)
    factor = lax.rsqrt(jnp.mean(wide * wide, axis=-1, keepdims=True) + eps_norm)
    return wide * factor * gain_vec


def angles(position, head_size):
    half_dim = head_size // 2
    frequency = rope_base ** (-jnp.arange(half_dim, dtype=jnp.float32) / half_dim)
    return position.astype(jnp.float32)[..., None] * frequency


def rotate_halves(vector, angle_arg):
    half_dim = vector.shape[-1] // 2
    lower_half = vector[..., :half_dim]
    upper_half = vector[..., half_dim:]
    cosine = jnp.cos(angle_arg)
    sine_part = jnp.sin(angle_arg)
    return jnp.concatenate(
        [
            lower_half * cosine - upper_half * sine_part,
            upper_half * cosine + lower_half * sine_part,
        ],
        axis=-1,
    )


def rotary_heads(raw_proj, gain_vec, position, head_count):
    head_size = gain_vec.shape[0]
    split_heads = raw_proj.reshape(raw_proj.shape[0], head_count, head_size)
    normed = norm_rows(split_heads, gain_vec)
    return rotate_halves(normed, angles(position, head_size)[:, None, :]).astype(jnp.bfloat16)


def merge_kernel(head, heads, groups, out_ref, lse_ref, q_ref, k_ref, v_ref, row_ref, col_ref,
                 done_ref, got_out, got_lse, fresh_acc, fresh_peak, fresh_total, merged,
                 send_out, recv_out, send_lse, recv_lse):
    n = out_ref.shape[0]
    me = lax.axis_index("req")
    chunks = q_ref.shape[0] // CHUNK
    scale = head ** (-0.5) * LOG2E

    barrier = pltpu.get_barrier_semaphore()
    for d in range(1, n):
        pl.semaphore_signal(
            barrier, inc=1, device_id={"req": lax.rem(me + d, n)}, device_id_type=MESH
        )
    pl.semaphore_wait(barrier, n - 1)

    copies = []
    for d in range(1, n):
        other = lax.rem(me + d, n)
        small = pltpu.make_async_remote_copy(
            src_ref=lse_ref.at[other], dst_ref=got_lse.at[d - 1], send_sem=send_lse.at[d - 1],
            recv_sem=recv_lse.at[d - 1], device_id={"req": other}, device_id_type=MESH,
        )
        small.start()
        copies.append(small)
    outs = []
    for d in range(1, n):
        other = lax.rem(me + d, n)
        large = pltpu.make_async_remote_copy(
            src_ref=out_ref.at[other], dst_ref=got_out.at[d - 1], send_sem=send_out.at[d - 1],
            recv_sem=recv_out.at[d - 1], device_id={"req": other}, device_id_type=MESH,
        )
        large.start()
        outs.append(large)

    for c in range(chunks):
        row = row_ref[:, c * CHUNK:(c + 1) * CHUNK]
        live = col_ref[...] <= jnp.concatenate([row] * groups, axis=1)
        for h in range(heads):
            at = h * chunks + c
            query = jnp.concatenate(
                [
                    q_ref[c * CHUNK:(c + 1) * CHUNK,
                          (h * groups + g) * head:(h * groups + g + 1) * head]
                    for g in range(groups)
                ],
                axis=0,
            )
            scores = lax.dot_general(
                k_ref[:, h * head:(h + 1) * head], query, (((1,), (1,)), ((), ())),
                preferred_element_type=jnp.float32,
            )
            scores = jnp.where(live, scores * scale, floor_score)
            top = jnp.max(scores, axis=0, keepdims=True)
            weights = jnp.exp2(scores - top)
            fresh_peak[at] = top
            fresh_total[at] = jnp.sum(weights, axis=0, keepdims=True)
            fresh_acc[at] = lax.dot_general(
                v_ref[:, h * head:(h + 1) * head], weights.astype(jnp.bfloat16),
                (((0,), (0,)), ((), ())), preferred_element_type=jnp.float32,
            )

    for small in copies:
        small.wait_recv()
    own_lse = lse_ref[me]
    columns = {}
    for h in range(heads):
        for c in range(chunks):
            at = h * chunks + c
            rows = [own_lse[at:at + 1, :]] + [got_lse[d - 1, at:at + 1, :] for d in range(1, n)]
            top = fresh_peak[at]
            for one in rows:
                top = jnp.maximum(top, one)
            fresh_factor = jnp.exp2(fresh_peak[at] - top)
            factors = [jnp.exp2(one - top) for one in rows]
            total = fresh_total[at] * fresh_factor
            for one in factors:
                total = total + one
            inverse = 1.0 / total
            stacked = jnp.concatenate(
                [one * inverse for one in factors]
                + [jnp.zeros((CHUNK - n, groups * CHUNK), jnp.float32)],
                axis=0,
            )
            columns[at] = stacked.T
            fresh = (fresh_acc[at] * (fresh_factor * inverse)).T
            for g in range(groups):
                at_rows = slice(c * CHUNK, (c + 1) * CHUNK)
                at_cols = slice((h * groups + g) * head, (h * groups + g + 1) * head)
                merged[at_rows, at_cols] = fresh[g * CHUNK:(g + 1) * CHUNK] + out_ref[
                    me, at_rows, at_cols
                ].astype(jnp.float32) * columns[at][g * CHUNK:(g + 1) * CHUNK, 0:1]
    for d in range(1, n):
        outs[d - 1].wait_recv()
        for h in range(heads):
            for c in range(chunks):
                at = h * chunks + c
                for g in range(groups):
                    at_rows = slice(c * CHUNK, (c + 1) * CHUNK)
                    at_cols = slice((h * groups + g) * head, (h * groups + g + 1) * head)
                    merged[at_rows, at_cols] += got_out[d - 1, at_rows, at_cols].astype(
                        jnp.float32
                    ) * columns[at][g * CHUNK:(g + 1) * CHUNK, d:d + 1]
    done_ref[...] = merged[...].astype(done_ref.dtype)
    for copy in copies + outs:
        copy.wait_send()


def exchange_and_merge(held_out, held_lse, queries, keys, values, position, head):
    n, rows, width = held_out.shape
    heads = keys.shape[1] // head
    groups = width // keys.shape[1]
    pairs = heads * (rows // CHUNK)
    vmem = pl.BlockSpec(memory_space=pltpu.VMEM)
    return pl.pallas_call(
        functools.partial(merge_kernel, head, heads, groups),
        out_shape=jax.ShapeDtypeStruct((rows, width), jnp.bfloat16),
        in_specs=[vmem] * 7,
        out_specs=vmem,
        scratch_shapes=[
            pltpu.VMEM((n - 1, rows, width), jnp.bfloat16),
            pltpu.VMEM((n - 1,) + held_lse.shape[1:], jnp.float32),
            pltpu.VMEM((pairs, head, groups * CHUNK), jnp.float32),
            pltpu.VMEM((pairs, 1, groups * CHUNK), jnp.float32),
            pltpu.VMEM((pairs, 1, groups * CHUNK), jnp.float32),
            pltpu.VMEM((rows, width), jnp.float32),
        ]
        + [pltpu.SemaphoreType.DMA((n - 1,))] * 4,
        compiler_params=pltpu.CompilerParams(
            collective_id=0, has_side_effects=True, vmem_limit_bytes=40 * 1024 * 1024
        ),
        name="exchange_and_merge",
    )(held_out, held_lse, queries, keys, values, position[None, :], position[:, None])


def group_sum_kernel(term_ref, base_ref, out_ref, pair_in, chip_sum, cross_in,
                     send_pair, recv_pair, send_cross, recv_cross, send_own, recv_own,
                     send_pass, recv_pass):
    chips = chip_sum.shape[0]
    rows = term_ref.shape[0]
    half = rows // 2
    part = half // chips
    me = lax.axis_index("tp")
    core = lax.rem(me, 2)
    chip = me // 2
    sibling = chip * 2 + 1 - core

    def same_core(d):
        return lax.rem(chip + d, chips)

    def rows_of(core_at, chip_at):
        return pl.ds(pl.multiple_of(core_at * half + chip_at * part, part), part)

    barrier = pltpu.get_barrier_semaphore()
    for d in range(1, chips):
        pl.semaphore_signal(
            barrier, inc=1, device_id={"tp": same_core(d) * 2 + core}, device_id_type=MESH
        )
    pl.semaphore_signal(barrier, inc=1, device_id={"tp": sibling}, device_id_type=MESH)
    pl.semaphore_wait(barrier, chips)

    order = list(range(1, chips)) + [0]
    pair = {}
    for d in order:
        chip_at = same_core(d)
        pair[d] = pltpu.make_async_remote_copy(
            src_ref=term_ref.at[rows_of(1 - core, chip_at)], dst_ref=pair_in.at[d],
            send_sem=send_pair.at[d], recv_sem=recv_pair.at[d],
            device_id={"tp": sibling}, device_id_type=MESH,
        )
        pair[d].start()
    cross = {}
    for d in range(1, chips):
        chip_at = same_core(d)
        pair[d].wait_recv()
        chip_sum[d] = (
            term_ref[rows_of(core, chip_at), :].astype(jnp.float32)
            + pair_in[d].astype(jnp.float32)
        ).astype(chip_sum.dtype)
        cross[d] = pltpu.make_async_remote_copy(
            src_ref=chip_sum.at[d], dst_ref=cross_in.at[d],
            send_sem=send_cross.at[d], recv_sem=recv_cross.at[d],
            device_id={"tp": chip_at * 2 + core}, device_id_type=MESH,
        )
        cross[d].start()
    pair[0].wait_recv()
    mine = rows_of(core, chip)
    summed = term_ref[mine, :].astype(jnp.float32) + pair_in[0].astype(jnp.float32)
    for d in range(1, chips):
        cross[d].wait_recv()
        summed = summed + cross_in[d].astype(jnp.float32)
    out_ref[mine, :] = (base_ref[mine, :].astype(jnp.float32) + summed).astype(out_ref.dtype)
    own = []
    for d in range(1, chips):
        own.append(
            pltpu.make_async_remote_copy(
                src_ref=out_ref.at[mine], dst_ref=out_ref.at[mine],
                send_sem=send_own.at[d], recv_sem=recv_own.at[d],
                device_id={"tp": same_core(d) * 2 + core}, device_id_type=MESH,
            )
        )
        own[-1].start()
    passed = []
    for d in range(chips):
        if d > 0:
            own[d - 1].wait_recv()
        come = rows_of(core, lax.rem(chip - d + chips, chips))
        passed.append(
            pltpu.make_async_remote_copy(
                src_ref=out_ref.at[come], dst_ref=out_ref.at[come],
                send_sem=send_pass.at[d], recv_sem=recv_pass.at[d],
                device_id={"tp": sibling}, device_id_type=MESH,
            )
        )
        passed[-1].start()
    for copy in passed:
        copy.wait_recv()
    for copy in list(pair.values()) + list(cross.values()) + own + passed:
        copy.wait_send()


def add_group_sum(term, base, collective_id):
    chips = lax.axis_size("tp") // 2
    rows, width = term.shape
    part = rows // 2 // chips
    vmem = pl.BlockSpec(memory_space=pltpu.VMEM)
    return pl.pallas_call(
        group_sum_kernel,
        out_shape=jax.ShapeDtypeStruct((rows, width), jnp.bfloat16),
        in_specs=[vmem] * 2,
        out_specs=vmem,
        scratch_shapes=[pltpu.VMEM((chips, part, width), jnp.bfloat16)] * 3
        + [pltpu.SemaphoreType.DMA((chips,))] * 8,
        compiler_params=pltpu.CompilerParams(
            collective_id=collective_id, has_side_effects=True, vmem_limit_bytes=32 * 1024 * 1024
        ),
        name="add_group_sum",
    )(term, base)


def swiglu(rows_in, w_gate, w_up):
    gate_proj = jnp.dot(rows_in, w_gate, preferred_element_type=jnp.float32)
    up_proj = jnp.dot(rows_in, w_up, preferred_element_type=jnp.float32)
    return (jax.nn.silu(gate_proj) * up_proj).astype(jnp.bfloat16)


def on_device(
    hidden_in,
    recompute_pos,
    req_lengths,
    stretch_order,
    page_table,
    cached_key_pool,
    cached_value_pool,
    attn_gain,
    w_query,
    w_key,
    value_weight,
    query_gain,
    key_norm_gain,
    w_out,
    ffn_gain,
    w_gate,
    w_up,
    w_down,
):
    req_count = lax.axis_size("req")
    my_index = lax.axis_index("req")
    head_size = query_gain.shape[0]
    query_heads = w_query.shape[1] // head_size
    key_heads = w_key.shape[1] // head_size
    count_of_rows = hidden_in.shape[0]
    local_reqs = REQ_DEV
    req_rows = RECOMPUTE_TOKENS
    entries = local_reqs * MOST_STRETCHES
    pair_cap = entries // req_count
    normed = norm_rows(hidden_in, attn_gain).astype(jnp.bfloat16)
    query_raw = jnp.dot(normed, w_query, preferred_element_type=jnp.float32)
    unnormed_keys = jnp.dot(normed, w_key, preferred_element_type=jnp.float32)
    recomputed_values = (
        jnp.dot(normed, value_weight, preferred_element_type=jnp.float32)
        .astype(jnp.bfloat16)
    )
    my_positions = lax.dynamic_slice_in_dim(recompute_pos, my_index * local_reqs, local_reqs, 0)
    flattened_position = my_positions.reshape(count_of_rows)
    queries = rotary_heads(query_raw, query_gain, flattened_position, query_heads)
    recomputed_keys = rotary_heads(unnormed_keys, key_norm_gain, flattened_position, key_heads)
    holder_table = page_table[0][stretch_order]
    slot_table = page_table[1][stretch_order]
    holder_hits = holder_table[:, :, None] == jnp.arange(req_count)[None, None, :]
    hit_counts = jnp.cumsum(holder_hits.astype(jnp.int32), axis=1)
    pair_rank = jnp.sum(jnp.where(holder_hits, hit_counts - 1, 0), axis=2)
    my_sends = (holder_table == my_index)[:, :, None] & (
        pair_rank[:, :, None] == jnp.arange(pair_cap)[None, None, :]
    )
    send_slot = jnp.sum(jnp.where(my_sends, slot_table[:, :, None], 0), axis=1)
    place_ids = jnp.arange(MOST_STRETCHES)[None, :, None]
    send_place = jnp.sum(jnp.where(my_sends, place_ids, 0), axis=1)
    below = jnp.sum(
        (recompute_pos[:, None, :] <= (send_place * STRETCH_TOKENS)[:, :, None]).astype(jnp.int32),
        axis=2,
    )
    first_row = jnp.where(send_place < req_lengths[:, None], below, req_rows)
    shift_angle = angles(jnp.arange(MOST_STRETCHES) * STRETCH_TOKENS, head_size)
    cosine, sine = jnp.cos(shift_angle), jnp.sin(shift_angle)
    queries_all = lax.all_gather(
        queries.reshape(count_of_rows, query_heads * head_size), "req", axis=0
    )
    held_out, held_lse = held_attention(
        queries_all,
        send_slot.reshape(-1),
        send_place.reshape(-1),
        first_row.reshape(-1),
        cached_key_pool,
        cached_value_pool,
        recompute_pos.reshape(req_count, 1, req_rows),
        jnp.concatenate([cosine, cosine], axis=1),
        jnp.concatenate([-sine, sine], axis=1),
    )
    attended = exchange_and_merge(
        held_out,
        held_lse,
        queries.reshape(count_of_rows, query_heads * head_size),
        recomputed_keys.reshape(count_of_rows, key_heads * head_size),
        recomputed_values,
        flattened_position,
        head_size,
    )
    attn_term = jnp.dot(attended, w_out, preferred_element_type=jnp.float32).astype(jnp.bfloat16)
    residual = add_group_sum(attn_term, hidden_in, 1)
    normed_ffn = norm_rows(residual, ffn_gain).astype(jnp.bfloat16)
    hidden = swiglu(normed_ffn, w_gate, w_up)
    ffn_term = jnp.dot(hidden, w_down, preferred_element_type=jnp.float32).astype(jnp.bfloat16)
    return add_group_sum(ffn_term, residual, 2)


def solution(mesh):
    return jax.shard_map(
        on_device,
        mesh=mesh,
        in_specs=(
            P("req", None),
            P(),
            P(),
            P(),
            P(),
            P("req", None, "tp"),
            P("req", None, "tp"),
            P(),
            P(None, "tp"),
            P(None, "tp"),
            P(None, "tp"),
            P(),
            P(),
            P("tp", None),
            P(),
            P(None, "tp"),
            P(None, "tp"),
            P("tp", None),
        ),
        out_specs=P("req", None),
        check_vma=False,
    )
```
